512 devices in a mesh: tm: 32 (over z, y_hi), sta: 16 (over x, y_lo, core).
Axes of the slice: x: 4, y: 4 (y_hi: 2, y_lo: 2; y = y_hi * 2 + y_lo), z: 16, core: 2. Of those that a mesh axis runs over, the one named last changes fastest.
Arguments:
- record: float32 [3072, 16384], P('sta', 'tm'), may hold values from -200 to 200
- owner: int32 [96, 1], replicated, may hold values from 0 to 31; in each aligned block of 32 rows (0 to 31, 32 to 63, ...) at most 2 rows name the same one
- offset: int32 [96], replicated, may hold values from 0 to 511
- station: int32 [3072], P('sta'), may hold values from 0 to 1023, as said below
- valid: int32 [3072], P('sta'), may hold values 0 or 1
Outputs:
- stack: float32 [3, 32, 16384], P(None, 'sta', 'tm')
The draws below stay inside these ranges and needn't reach their ends.
Inputs may be any that keep to these rules, and one draw needn't show every extreme that they name: `owner`: among the 32 templates of one step (rows i * 32 to i * 32 + 31) no time block is named more than 2 times, and some block is named exactly 2 times in some step. Every station number names exactly 3 channels.
All inputs are finite; a program needn't handle non-finite values. No bound on the sum of `valid` on one device may be relied on, other than what follows from the above.
Results may differ from the reference program's by a relative error of at most 0.0015.
Values may be sent and summed in bfloat16 or wider, within the bound.
No kernel may reach another device: no remote copies, remote signals or barrier semaphores. Data moves between devices by JAX's collectives and lax.ppermute only.
A program may use at most 64 MiB of HBM per device.

```python
import math
import jax
import jax.numpy as jnp
import numpy as np
from jax import lax

WIN = 100
S_DEV = 512
TPL_STEP = 32
NSTEP = 3
NTPL = 96
CHANNELS = 3072
SAMPLES = 16384
NSTATIONS = 1024
MOST = 2
N_TM = 32


def draw_record(key, part):
    noise_key, gain_key, envelope_key = jax.random.split(key, 3)
    noise = jnp.clip(jax.random.normal(noise_key, (CHANNELS, SAMPLES), jnp.float32), -6.0, 6.0)
    gains = jnp.exp(jax.random.uniform(gain_key, (CHANNELS, 1), jnp.float32, 0.0, math.log(10.0)))
    envelope = jnp.exp(jax.random.uniform(envelope_key, (CHANNELS, SAMPLES // 32, 1), jnp.float32, -1.0, 1.0))
    envelope = jnp.broadcast_to(envelope, (CHANNELS, SAMPLES // 32, 32)).reshape(CHANNELS, SAMPLES)
    return (noise * gains * envelope).astype(jnp.float32)


def draw_station(key, part):
    shuffled = jax.random.permutation(key, CHANNELS)
    return (shuffled // 3).astype(jnp.int32)


def place_ends(entries, own_key, least, high):
    index_at = [jax.random.randint(jax.random.fold_in(own_key, axis), (), 0, length) for axis, length in enumerate(entries.shape)]
    main_axis = entries.shape.index(max(entries.shape))
    beside = index_at[:main_axis] + [(index_at[main_axis] + 1) % entries.shape[main_axis]] + index_at[main_axis + 1:]
    return entries.at[tuple(index_at)].set(least).at[tuple(beside)].set(high)


def routed_block(rng, own, number, rows, amount, top, bound, skew):
    order = jax.random.permutation(rng, amount)
    packed, ordinary = shares(amount, rows * top, bound, skew, True), shares(amount, rows * top, bound, skew, False)
    places = jnp.arange(amount)

    def named(sizes, turn):
        used = int((sizes > 0).sum())
        fixed = max(1, used // 4)
        moved = fixed + (places - fixed + turn * (used - fixed)) % max(1, amount - fixed)
        return jnp.zeros((amount,), jnp.int32).at[order[jnp.where(places < fixed, places, moved)]].set(jnp.asarray(sizes, jnp.int32))

    sizes = jnp.where(number % 4 == 0, named(packed, number // 4), named(ordinary, number - number // 4 - 1))
    mixed = jax.random.permutation(jax.random.fold_in(own, 3), amount)
    source_of, sink = mixed[0:amount // 2 * 2:2], mixed[1:amount // 2 * 2:2]
    margin = jnp.minimum(sizes[source_of] - 1, bound - sizes[sink]) // 2
    margin = jnp.where((source_of == order[0]) | (sink == order[0]) | (sizes[sink] == 0), 0, jnp.maximum(margin, 0))
    moved = jax.random.randint(jax.random.fold_in(own, 4), (amount // 2,), 0, 1 << 20) % (margin + 1)
    sizes = sizes.at[source_of].add(-moved).at[sink].add(moved)
    labels = jnp.searchsorted(jnp.cumsum(sizes), jnp.arange(rows * top), side="right").astype(jnp.int32)
    table = labels.reshape(top, rows).T
    table = table[jax.random.permutation(jax.random.fold_in(own, 1), rows)]
    turn = jax.random.randint(jax.random.fold_in(own, 2), (rows, 1), 0, top)
    return jnp.take_along_axis(table, (jnp.arange(top)[None, :] + turn) % top, axis=1)


def shares(number_of, total, most, skew, full):
    portions = [(1 << 20) // math.isqrt(standing ** skew) + 1 for standing in range(1, number_of + 1)]
    largest = most if full else min(most, max(-(-total // number_of), total * portions[0] // sum(portions)))
    least = 1 if total - largest >= number_of - 1 else 0
    given, rest = [largest] + [least] * (number_of - 1), total - largest - least * (number_of - 1)
    while rest > 0:
        candidates = [i for i in range(1, number_of) if given[i] < largest] or [i for i in range(1, number_of) if given[i] < most]
        pool, left = sum([portions[i] for i in candidates]), rest
        for i in candidates:
            more = min(most - given[i], max(1, left * portions[i] // pool), rest)
            given[i] = given[i] + more
            rest = rest - more
    return np.array(given)


def setup_inputs(seed: int = 0) -> dict:
    splits = jax.random.split(jax.random.key(seed), 6)
    record = draw_record(jax.random.fold_in(splits[5], 71), 0)
    owner_keys = jax.random.split(jax.random.fold_in(splits[1], 1), NTPL // TPL_STEP)
    owner_turns = jax.random.permutation(jax.random.fold_in(splits[1], 3), NTPL // TPL_STEP)
    owner = jax.vmap(lambda own, number: routed_block(jax.random.fold_in(splits[1], 2), own, number, TPL_STEP, N_TM, 1, MOST, 2))(owner_keys, owner_turns).reshape((NTPL, 1))
    offset = place_ends(jax.random.randint(splits[2], (NTPL,), 0, S_DEV), jax.random.fold_in(splits[2], 1), 0, S_DEV - 1).astype(jnp.int32)
    station = draw_station(jax.random.fold_in(splits[5], 71), 0)
    valid = place_ends((jax.random.randint(splits[4], (CHANNELS,), 0, 5) < 4).astype(jnp.int32), jax.random.fold_in(splits[4], 1), 0, 1)
    return {"record": record, "owner": owner, "offset": offset, "station": station, "valid": valid}


EPSILON = 1e-05

def normalize(pieces):
    values = pieces.astype(jnp.float32)
    centred = values - lax.optimization_barrier(jnp.mean(values, axis=-1, keepdims=True))
    spread = jnp.sqrt(lax.optimization_barrier(jnp.mean(centred * centred, axis=-1, keepdims=True)) + EPSILON)
    return (centred / (WIN * spread)).astype(jnp.bfloat16)

def reference(record, owner, offset, station, valid):
    extended = jnp.concatenate([record.astype(jnp.bfloat16), jnp.zeros((CHANNELS, WIN - 1), jnp.bfloat16)], axis=1)
    starts = owner[:, 0].astype(jnp.int32) * SAMP_FACTOR_FIX(S_DEV) + offset.astype(jnp.int32)

    def template_at(first_sample):
        return lax.dynamic_slice_in_dim(extended, first_sample, WIN, 1)
    templates = normalize(lax.map(template_at, starts))
    present = valid.astype(jnp.float32)
    counts = jax.ops.segment_sum(present, station.astype(jnp.int32), num_segments=NSTATIONS)
    weight = present / jnp.maximum(counts[station.astype(jnp.int32)], 1.0)
    block_size = 8
    block_count = CHANNELS // block_size

    def add_block(running, block_index):
        channel_rows = lax.dynamic_slice_in_dim(extended, block_index * block_size, block_size, 0)
        hankel = jnp.stack([channel_rows[:, k:k + SAMPLES] for k in range(WIN)], axis=1)
        values = hankel.astype(jnp.float32)
        window_mean = lax.optimization_barrier(jnp.mean(values, axis=1))
        window_square = lax.optimization_barrier(jnp.mean(values * values, axis=1))
        inverse = 1.0 / jnp.sqrt(jnp.maximum(window_square - window_mean * window_mean, 0.0) + EPSILON)
        scaled = lax.dynamic_slice_in_dim(weight, block_index * block_size, block_size, 0)
        window = (values * (scaled[:, None] * inverse)[:, None, :]).astype(jnp.bfloat16)
        template_part = lax.dynamic_slice_in_dim(templates, block_index * block_size, block_size, 1)
        template_part = template_part.reshape(NTPL, block_size * WIN)
        product = jnp.dot(template_part, window.reshape(block_size * WIN, SAMPLES), preferred_element_type=jnp.float32)
        return (running + product, None)
    running, unused = lax.scan(add_block, jnp.zeros((NTPL, SAMPLES), jnp.float32), jnp.arange(block_count, dtype=jnp.int32))
    result = running / math.sqrt(NSTATIONS)
    return result.reshape(NSTEP, TPL_STEP, SAMPLES)

def SAMP_FACTOR_FIX(value):
    return value
```

```python
import functools

import jax
import jax.numpy as jnp
from jax import lax
from jax.experimental import pallas as pl
from jax.experimental.pallas import tpu as pltpu
from jax.sharding import Mesh
from jax.sharding import PartitionSpec as P

WIN = 100
EPSILON = 1e-05
NTPL = 96
NSTEP = 3
TPL_STEP = 32
BLOCK = 512
LANES = 128
BASE = 16
GROUPS = 7

FAR = ("zh",)
NEAR = ("zl", "yh")
TM = FAR + NEAR
STA = ("x", "yl", "core")


def shift_left(value, by):
    if by == 0:
        return value
    return pltpu.roll(value, value.shape[1] - by, axis=1)


def correlate(
    group_ref, start_ref, rec_ref, codes_ref, own_ref, out_ref,
    tiles, ext, raw, tmat, base32, base16, scale, win, acc,
):
    blocks, chans, _ = rec_ref.shape
    n_near = ext.shape[1] // BLOCK
    samples = n_near * BLOCK
    wide = samples + LANES
    group = group_ref[0]
    per_block = BLOCK // LANES

    def copy_block(b, carry):
        values = rec_ref[b].astype(jnp.float32)
        for q in range(per_block):
            tiles[b * per_block + q] = values[:, q * LANES : (q + 1) * LANES]
        return carry

    lax.fori_loop(0, blocks, copy_block, 0)
    tiles[blocks * per_block] = jnp.zeros((chans, LANES), jnp.float32)

    first_tile = group * (n_near * per_block)
    for q in range(n_near * per_block + 1):
        ext[:, q * LANES : (q + 1) * LANES] = tiles[first_tile + q]

    def take_template(row, carry):
        start = start_ref[row]
        tile = start // LANES
        rest = start - tile * LANES
        back = lax.rem(LANES - rest, LANES)
        low = pltpu.roll(tiles[tile], back, axis=1)
        high = pltpu.roll(tiles[tile + 1], back, axis=1)
        lane = lax.broadcasted_iota(jnp.int32, (chans, LANES), 1)
        raw[pl.ds(row, chans, stride=NTPL), :] = jnp.where(lane < LANES - rest, low, high)
        return carry

    lax.fori_loop(0, NTPL, take_template, 0, unroll=8)

    lane = lax.broadcasted_iota(jnp.int32, (NTPL, LANES), 1)
    inside = lane < WIN
    for c in range(chans):
        values = jnp.where(inside, raw[c * NTPL : (c + 1) * NTPL, :], 0.0)
        mean = jnp.sum(values, axis=1, keepdims=True) / WIN
        centred = jnp.where(inside, values - mean, 0.0)
        spread = jnp.sqrt(jnp.sum(centred * centred, axis=1, keepdims=True) / WIN + EPSILON)
        tmat[:, c * LANES : (c + 1) * LANES] = (centred / (WIN * spread)).astype(jnp.bfloat16)

    codes = codes_ref[...].astype(jnp.int32)
    own = own_ref[...].astype(jnp.int32)
    own_station = own // 2
    own_valid = own - own_station * 2
    counts = jnp.zeros((chans, LANES), jnp.int32)
    for r in range(codes.shape[0]):
        row = codes[r : r + 1, :]
        station = row // 2
        counts = counts + jnp.where(own_station == station, row - station * 2, 0)
    total = jnp.sum(counts.astype(jnp.float32), axis=1, keepdims=True)
    weight = own_valid.astype(jnp.float32) / jnp.maximum(total, 1.0)

    values = ext[...]

    def window_sum(v):
        two = v + shift_left(v, 1)
        four = two + shift_left(two, 2)
        eight = four + shift_left(four, 4)
        sixteen = eight + shift_left(eight, 8)
        most = sixteen + shift_left(sixteen, 16)
        most64 = most + shift_left(most, 32)
        return most64 + shift_left(most, 64) + shift_left(four, 96)

    mean = window_sum(values) / WIN
    square = window_sum(values * values) / WIN
    inverse = 1.0 / jnp.sqrt(jnp.maximum(square - mean * mean, 0.0) + EPSILON)
    scale[...] = (weight * inverse)[:, :samples]

    for q in range(n_near * per_block + 1):
        low = tiles[first_tile + q]
        high = tiles[jnp.minimum(first_tile + q + 1, blocks * per_block)]
        pair = jnp.concatenate([low, high], axis=1)
        for i in range(BASE):
            base32[pl.ds(i, chans, stride=BASE), :] = shift_left(pair, i)[:, :LANES]
        base16[q] = base32[...].astype(jnp.bfloat16)

    for c in range(chans):
        win[c * LANES + GROUPS * BASE : (c + 1) * LANES, :] = jnp.zeros(
            (LANES - GROUPS * BASE, BLOCK), jnp.bfloat16
        )

    def one_block(e, carry):
        first = pl.multiple_of(e * BLOCK, BLOCK)

        def one_channel(c, inner):
            rows = pl.ds(pl.multiple_of(c * BASE, BASE), BASE)
            piece = jnp.concatenate(
                [base16[e * per_block + q, rows, :] for q in range(per_block + 1)], axis=1
            )
            factor = scale[pl.ds(c, 1), pl.ds(first, BLOCK)]
            for g in range(GROUPS):
                moved = shift_left(piece, g * BASE)[:, :BLOCK]
                win[pl.ds(pl.multiple_of(c * LANES + g * BASE, BASE), BASE), :] = (
                    moved.astype(jnp.float32) * factor
                ).astype(jnp.bfloat16)
            return inner

        lax.fori_loop(0, chans, one_channel, 0, unroll=2)
        product = jnp.dot(tmat[...], win[...], preferred_element_type=jnp.float32)
        n_sta = out_ref.shape[0]
        per_sta = NTPL // n_sta
        for r in range(per_sta):
            for q in range(per_block):
                acc[q, pl.ds(e * per_sta + r, n_sta, stride=n_near * per_sta), :] = product[
                    r * n_sta : (r + 1) * n_sta, q * LANES : (q + 1) * LANES
                ]
        return carry

    lax.fori_loop(0, n_near, one_block, 0)
    rows = n_near * NTPL // out_ref.shape[0]
    for j in range(out_ref.shape[0]):
        for q in range(per_block):
            out_ref[j, :, q * LANES : (q + 1) * LANES] = acc[q, j * rows : (j + 1) * rows, :].astype(
                jnp.bfloat16
            )


def body(record, owner, offset, station, valid):
    ch_dev, samp_dev = record.shape
    n_far, n_near, n_sta = lax.axis_size(FAR), lax.axis_size(NEAR), lax.axis_size(STA)
    chans = ch_dev // n_near
    per_sta = NTPL // n_sta

    code = (station * 2 + valid).astype(jnp.float32)
    codes = lax.all_to_all(
        jnp.broadcast_to(code[None, :], (n_sta, ch_dev)), STA, 0, 0, tiled=True
    ).reshape(n_sta * ch_dev // LANES, LANES)
    own = lax.dynamic_slice_in_dim(code, lax.axis_index(NEAR) * chans, chans)[:, None]

    rounded = record.astype(jnp.bfloat16).reshape(n_near, chans, samp_dev)
    mine = lax.all_to_all(rounded, NEAR, 0, 0, tiled=True)
    whole = lax.all_gather(mine, FAR, axis=0, tiled=True)

    starts = owner[:, 0] * samp_dev + offset
    starts = starts.reshape(NSTEP, n_sta, per_sta // NSTEP).transpose(0, 2, 1).reshape(NTPL)
    group = lax.axis_index(FAR).astype(jnp.int32).reshape(1)

    samples = n_near * samp_dev
    wide = samples + LANES
    smem = pl.BlockSpec(memory_space=pltpu.SMEM)
    vmem = pl.BlockSpec(memory_space=pltpu.VMEM)
    f32, bf16 = jnp.float32, jnp.bfloat16
    part = pl.pallas_call(
        correlate,
        out_shape=jax.ShapeDtypeStruct((n_sta, n_near * per_sta, samp_dev), bf16),
        in_specs=[smem, smem, vmem, vmem, vmem],
        out_specs=vmem,
        scratch_shapes=[
            pltpu.VMEM((n_far * n_near * samp_dev // LANES + 1, chans, LANES), f32),
            pltpu.VMEM((chans, wide), f32),
            pltpu.VMEM((chans * NTPL, LANES), f32),
            pltpu.VMEM((NTPL, chans * LANES), bf16),
            pltpu.VMEM((chans * BASE, LANES), f32),
            pltpu.VMEM((wide // LANES, chans * BASE, LANES), bf16),
            pltpu.VMEM((chans, samples), f32),
            pltpu.VMEM((chans * LANES, samp_dev), bf16),
            pltpu.VMEM((samp_dev // LANES, n_near * NTPL, LANES), f32),
        ],
        compiler_params=pltpu.CompilerParams(vmem_limit_bytes=48 * 1024 * 1024),
        cost_estimate=pl.CostEstimate(
            flops=2 * NTPL * chans * LANES * samples, bytes_accessed=2 << 20, transcendentals=0
        ),
    )(group, starts, whole, codes, own)

    moved = lax.all_to_all(part, STA, 0, 0, tiled=True)
    summed = jnp.sum(moved.astype(f32), axis=0).reshape(n_near, per_sta, samp_dev)
    last = lax.all_to_all(summed, NEAR, 0, 0, tiled=True)
    result = jnp.sum(last, axis=0) * (1.0 / 32.0)
    return result.reshape(NSTEP, per_sta // NSTEP, samp_dev)


def solution(mesh):
    fine = Mesh(mesh.devices.reshape(4, 4, 2, 4, 2, 2), TM + STA)
    placed = (P(STA, TM), P(), P(), P(STA), P(STA))
    return jax.shard_map(
        body, mesh=fine, in_specs=placed, out_specs=P(None, STA, TM), check_vma=False
    )
```

```python
import jax
import jax.numpy as jnp
from jax import lax
from jax.experimental import pallas as pl
from jax.experimental.pallas import tpu as pltpu
from jax.sharding import Mesh
from jax.sharding import PartitionSpec as P

WIN = 100
EPSILON = 1e-05
NTPL = 96
NSTEP = 3
TPL_STEP = 32
BLOCK = 512
LANES = 128
PER_BLOCK = BLOCK // LANES
BASE = 16
GROUPS = 7

RUN = 8
TM = ("zh", "zl", "yh")
SPLIT = ("zl", "yh")
GATHER = "zh"
STA = ("x", "yl", "core")

SMEM = pl.BlockSpec(memory_space=pltpu.SMEM)
VMEM = pl.BlockSpec(memory_space=pltpu.VMEM)
F32, BF16 = jnp.float32, jnp.bfloat16


def shift_left(value, by):
    if by == 0:
        return value
    return pltpu.roll(value, value.shape[1] - by, axis=1)


def deviations(values):
    def window_sum(v):
        two = v + shift_left(v, 1)
        four = two + shift_left(two, 2)
        eight = four + shift_left(four, 4)
        sixteen = eight + shift_left(eight, 8)
        half = sixteen + shift_left(sixteen, 16)
        whole = half + shift_left(half, 32)
        return whole + shift_left(half, 64) + shift_left(four, 96)

    mean = window_sum(values) / WIN
    square = window_sum(values * values) / WIN
    return 1.0 / jnp.sqrt(jnp.maximum(square - mean * mean, 0.0) + EPSILON)


def shifted_base(tile, n_tiles, base32, base16):
    chans = tile(0).shape[0]
    lane = lax.broadcasted_iota(jnp.int32, (chans, LANES), 1)
    low = [shift_left(tile(0), i) for i in range(BASE)]
    for q in range(n_tiles):
        if q < n_tiles - 1:
            high = [shift_left(tile(q + 1), i) for i in range(BASE)]
        else:
            high = [jnp.zeros((chans, LANES), F32)] * BASE
        for i in range(BASE):
            base32[pl.ds(i, chans, stride=BASE), :] = jnp.where(lane < LANES - i, low[i], high[i])
        base16[q] = base32[...].astype(BF16)
        low = high


def fill_windows(base16, first, count, factor, store):
    chans = base16.shape[1] // BASE
    for c in range(chans):
        piece = jnp.concatenate(
            [base16[first + q, c * BASE : (c + 1) * BASE, :] for q in range(count + 1)], axis=1
        )
        for g in range(GROUPS):
            moved = shift_left(piece, g * BASE)[:, : count * LANES]
            store(c * LANES + g * BASE, (moved.astype(F32) * factor(c)).astype(BF16))


def stack_kernel(
    group_ref, start_ref, rec_ref, codes_ref, own_ref, out_ref,
    tiles, ext, raw, tmat, base32, base16, scale, win0, win1, acc,
):
    n_gather, n_split, chans, _ = rec_ref.shape
    n_sta = out_ref.shape[0]
    per_sta = NTPL // n_sta
    n_runs = n_split // RUN
    run_tiles = RUN * PER_BLOCK + 1

    for l in range(n_gather):
        for h in range(n_runs):
            for y in range(RUN):
                block = (h * n_gather + l) * RUN + y
                for q in range(PER_BLOCK):
                    tiles[block * PER_BLOCK + q] = rec_ref[
                        l, h * RUN + y, :, q * LANES : (q + 1) * LANES
                    ].astype(F32)
    tiles[n_gather * n_split * PER_BLOCK] = jnp.zeros((chans, LANES), F32)

    for h in range(n_runs):
        first = (h * n_gather + group_ref[0]) * (RUN * PER_BLOCK)
        for q in range(run_tiles):
            place = (h * run_tiles + q) * LANES
            ext[:, place : place + LANES] = tiles[first + q]
    scale[...] = deviations(ext[...])
    shifted_base(
        lambda q: ext[:, q * LANES : (q + 1) * LANES], n_runs * run_tiles, base32, base16
    )

    def take_template(row, carry):
        start = start_ref[row]
        tile = start // LANES
        rest = start - tile * LANES
        back = lax.rem(LANES - rest, LANES)
        low = pltpu.roll(tiles[tile], back, axis=1)
        high = pltpu.roll(tiles[tile + 1], back, axis=1)
        lane = lax.broadcasted_iota(jnp.int32, (chans, LANES), 1)
        raw[pl.ds(row, chans, stride=NTPL), :] = jnp.where(lane < LANES - rest, low, high)
        return carry

    lax.fori_loop(0, NTPL, take_template, 0, unroll=16)

    codes = codes_ref[...].astype(jnp.int32)
    own = own_ref[...].astype(jnp.int32)
    own_station = own // 2
    own_valid = own - own_station * 2
    counts = jnp.zeros((chans, codes.shape[1]), jnp.int32)
    for r in range(codes.shape[0]):
        row = codes[r : r + 1, :]
        station = row // 2
        counts = counts + jnp.where(own_station == station, row - station * 2, 0)
    total = jnp.sum(counts.astype(F32), axis=1, keepdims=True)
    weight = own_valid.astype(F32) / jnp.maximum(total, 1.0)

    lane = lax.broadcasted_iota(jnp.int32, (NTPL, LANES), 1)
    inside = lane < WIN
    for c in range(chans):
        values = jnp.where(inside, raw[c * NTPL : (c + 1) * NTPL, :], 0.0)
        mean = jnp.sum(values, axis=1, keepdims=True) / WIN
        centred = jnp.where(inside, values - mean, 0.0)
        spread = jnp.sqrt(jnp.sum(centred * centred, axis=1, keepdims=True) / WIN + EPSILON)
        scaled = centred * (weight[c : c + 1, :] / (WIN * spread))
        tmat[:, c * LANES : (c + 1) * LANES] = scaled.astype(BF16)

    spare = jnp.zeros((LANES - GROUPS * BASE, BLOCK), BF16)
    for win in (win0, win1):
        for c in range(chans):
            win[c * LANES + GROUPS * BASE : (c + 1) * LANES, :] = spare

    def fill(e, win):
        first = e // RUN * run_tiles + e % RUN * PER_BLOCK
        lanes = pl.ds(pl.multiple_of(first * LANES, LANES), BLOCK)

        def store(row, values):
            win[row : row + BASE, :] = values

        fill_windows(base16, first, PER_BLOCK, lambda c: scale[c : c + 1, lanes], store)

    def multiply(e, win):
        product = jnp.dot(tmat[...], win[...], preferred_element_type=F32)
        for r in range(per_sta):
            for q in range(PER_BLOCK):
                acc[q, pl.ds(e * per_sta + r, n_sta, stride=n_split * per_sta), :] = product[
                    r * n_sta : (r + 1) * n_sta, q * LANES : (q + 1) * LANES
                ]

    fill(0, win0)

    def two_blocks(i, carry):
        multiply(2 * i, win0)
        fill(2 * i + 1, win1)
        multiply(2 * i + 1, win1)
        fill(2 * i + 2, win0)
        return carry

    lax.fori_loop(0, n_split // 2 - 1, two_blocks, 0)
    multiply(n_split - 2, win0)
    fill(n_split - 1, win1)
    multiply(n_split - 1, win1)
    rows = n_split * per_sta
    for j in range(n_sta):
        for q in range(PER_BLOCK):
            out_ref[j, :, q * LANES : (q + 1) * LANES] = acc[
                q, j * rows : (j + 1) * rows, :
            ].astype(BF16)


def body(record, owner, offset, station, valid):
    ch_dev, samp_dev = record.shape
    n_gather, n_split, n_sta = lax.axis_size(GATHER), lax.axis_size(SPLIT), lax.axis_size(STA)
    chans = ch_dev // n_split
    per_sta = NTPL // n_sta
    runs = n_split // RUN
    wide = runs * (RUN * PER_BLOCK + 1) * LANES

    code = (station * 2 + valid).astype(F32)
    codes = lax.all_to_all(
        jnp.broadcast_to(code[None, :], (n_sta, ch_dev)), STA, 0, 0, tiled=True
    ).reshape(n_sta * ch_dev // LANES, LANES)
    own = lax.dynamic_slice_in_dim(code, lax.axis_index(SPLIT) * chans, chans)[:, None]

    rounded = record.astype(BF16).reshape(n_split, chans, samp_dev)
    mine = lax.all_to_all(rounded, SPLIT, 0, 0, tiled=True)
    whole = lax.all_gather(mine, GATHER, axis=0, tiled=False)

    starts = owner[:, 0] * samp_dev + offset
    starts = starts.reshape(NSTEP, n_sta, per_sta // NSTEP).transpose(0, 2, 1).reshape(NTPL)
    group = lax.axis_index(GATHER).astype(jnp.int32).reshape(1)

    part = pl.pallas_call(
        stack_kernel,
        out_shape=jax.ShapeDtypeStruct((n_sta, n_split * per_sta, samp_dev), BF16),
        in_specs=[SMEM, SMEM, VMEM, VMEM, VMEM],
        out_specs=VMEM,
        scratch_shapes=[
            pltpu.VMEM((n_gather * n_split * PER_BLOCK + 1, chans, LANES), F32),
            pltpu.VMEM((chans, wide), F32),
            pltpu.VMEM((chans * NTPL, LANES), F32),
            pltpu.VMEM((NTPL, chans * LANES), BF16),
            pltpu.VMEM((chans * BASE, LANES), F32),
            pltpu.VMEM((wide // LANES, chans * BASE, LANES), BF16),
            pltpu.VMEM((chans, wide), F32),
            pltpu.VMEM((chans * LANES, samp_dev), BF16),
            pltpu.VMEM((chans * LANES, samp_dev), BF16),
            pltpu.VMEM((PER_BLOCK, n_split * NTPL, LANES), F32),
        ],
        compiler_params=pltpu.CompilerParams(vmem_limit_bytes=48 * 1024 * 1024),
        cost_estimate=pl.CostEstimate(
            flops=14_000_000_000, bytes_accessed=2 << 20, transcendentals=0
        ),
    )(group, starts, whole, codes, own)

    moved = lax.all_to_all(part, STA, 0, 0, tiled=True)
    summed = jnp.sum(moved.astype(F32), axis=0).reshape(n_split, per_sta, samp_dev)
    final = lax.all_to_all(summed, SPLIT, 0, 0, tiled=True)
    result = jnp.sum(final, axis=0) * (1.0 / 32.0)
    return result.reshape(NSTEP, per_sta // NSTEP, samp_dev)


def solution(mesh):
    fine = Mesh(mesh.devices.reshape(4, 4, 2, 4, 2, 2), TM + STA)
    placed = (P(STA, TM), P(), P(), P(STA), P(STA))
    return jax.shard_map(
        body, mesh=fine, in_specs=placed, out_specs=P(None, STA, TM), check_vma=False
    )
```

```python
import jax
import jax.numpy as jnp
from jax import lax
from jax.experimental import pallas as pl
from jax.experimental.pallas import tpu as pltpu
from jax.sharding import Mesh
from jax.sharding import PartitionSpec as P

WIN = 100
EPSILON = 1e-05
NTPL = 96
NSTEP = 3
TPL_STEP = 32
BLOCK = 512
LANES = 128
PER_BLOCK = BLOCK // LANES
BASE = 16
GROUPS = 7

RUN = 8
TM = ("zh", "zl", "yh")
SPLIT = ("zl", "yh")
GATHER = "zh"
STA = ("x", "yl", "core")

SMEM = pl.BlockSpec(memory_space=pltpu.SMEM)
VMEM = pl.BlockSpec(memory_space=pltpu.VMEM)
F32, BF16 = jnp.float32, jnp.bfloat16


def shift_left(value, by):
    if by == 0:
        return value
    return pltpu.roll(value, value.shape[1] - by, axis=1)


def dot(left, right):
    return jnp.dot(left.astype(BF16), right, preferred_element_type=F32)


def two_parts(value):
    high = value.astype(BF16)
    return high, value - high.astype(F32)


def deviations(values):
    n_tiles, chans, _ = values.shape
    flat = values.reshape(n_tiles * chans, LANES)
    row = lax.broadcasted_iota(jnp.int32, (LANES, LANES), 0)
    lane = lax.broadcasted_iota(jnp.int32, (LANES, LANES), 1)
    own = ((row >= lane) & (row < lane + WIN)).astype(F32).astype(BF16)
    after = (row + LANES < lane + WIN).astype(F32).astype(BF16)

    def window_sum(parts):
        here = sum(dot(part, own) for part in parts).reshape(n_tiles, chans, LANES)
        there = sum(dot(part, after) for part in parts).reshape(n_tiles, chans, LANES)
        return here[:-1] + there[1:]

    mean = window_sum([flat]) / WIN
    square = window_sum(two_parts(flat * flat)) / WIN
    return 1.0 / jnp.sqrt(jnp.maximum(square - mean * mean, 0.0) + EPSILON)


def shifted_base(tile, n_tiles, base32, base16, place):
    chans = tile(0).shape[0]
    lane = lax.broadcasted_iota(jnp.int32, (chans, LANES), 1)
    low = [shift_left(tile(0), i) for i in range(BASE)]
    for q in range(n_tiles):
        if q < n_tiles - 1:
            high = [shift_left(tile(q + 1), i) for i in range(BASE)]
        else:
            high = [jnp.zeros((chans, LANES), F32)] * BASE
        for i in range(BASE):
            base32[pl.ds(i, chans, stride=BASE), :] = jnp.where(lane < LANES - i, low[i], high[i])
        base16[place + q] = base32[...].astype(BF16)
        low = high


def fill_windows(base16, first, count, factor, store):
    chans = base16.shape[1] // BASE
    for c in range(chans):
        piece = jnp.concatenate(
            [base16[first + q, c * BASE : (c + 1) * BASE, :] for q in range(count + 1)], axis=1
        )
        for g in range(GROUPS):
            moved = shift_left(piece, g * BASE)[:, : count * LANES]
            store(c * LANES + g * BASE, (moved.astype(F32) * factor(c)).astype(BF16))


def stack_kernel(
    group_ref, start_ref, rec_ref, codes_ref, own_ref, out_ref,
    tiles, raw, tmat, base32, base16, scale, win0, win1, acc,
):
    n_gather, n_split, chans, _ = rec_ref.shape
    n_sta = out_ref.shape[0]
    per_sta = NTPL // n_sta
    n_runs = n_split // RUN
    run_tiles = RUN * PER_BLOCK + 1

    for l in range(n_gather):
        for h in range(n_runs):
            for y in range(RUN):
                block = (h * n_gather + l) * RUN + y
                for q in range(PER_BLOCK):
                    tiles[block * PER_BLOCK + q] = rec_ref[
                        l, h * RUN + y, :, q * LANES : (q + 1) * LANES
                    ].astype(F32)
    tiles[n_gather * n_split * PER_BLOCK] = jnp.zeros((chans, LANES), F32)

    codes = codes_ref[...].astype(jnp.int32)
    own = own_ref[...].astype(jnp.int32)
    own_station = own // 2
    own_valid = own - own_station * 2
    counts = jnp.zeros((chans, codes.shape[1]), jnp.int32)
    for r in range(codes.shape[0]):
        row = codes[r : r + 1, :]
        station = row // 2
        counts = counts + jnp.where(own_station == station, row - station * 2, 0)
    total = jnp.sum(counts.astype(F32), axis=1, keepdims=True)
    weight = own_valid.astype(F32) / jnp.maximum(total, 1.0)

    for h in range(n_runs):
        first = (h * n_gather + group_ref[0]) * (RUN * PER_BLOCK)
        values = tiles[pl.ds(first, run_tiles)]
        scale[h * run_tiles : (h + 1) * run_tiles - 1] = weight[None] * deviations(values)
        shifted_base(lambda q: tiles[first + q], run_tiles, base32, base16, h * run_tiles)

    def take_template(row, carry):
        start = start_ref[row]
        tile = start // LANES
        rest = start - tile * LANES
        back = lax.rem(LANES - rest, LANES)
        low = pltpu.roll(tiles[tile], back, axis=1)
        high = pltpu.roll(tiles[tile + 1], back, axis=1)
        lane = lax.broadcasted_iota(jnp.int32, (chans, LANES), 1)
        raw[pl.ds(row, chans, stride=NTPL), :] = jnp.where(lane < LANES - rest, low, high)
        return carry

    lax.fori_loop(0, NTPL, take_template, 0, unroll=96)

    lane = lax.broadcasted_iota(jnp.int32, (NTPL, LANES), 1)
    inside = lane < WIN
    ones = jnp.ones((LANES, LANES), BF16)
    for c in range(chans):
        values = jnp.where(inside, raw[c * NTPL : (c + 1) * NTPL, :], 0.0)
        mean = dot(values, ones) / WIN
        centred = jnp.where(inside, values - mean, 0.0)
        total = sum(dot(part, ones) for part in two_parts(centred * centred))
        spread = jnp.sqrt(total / WIN + EPSILON)
        tmat[:, c * LANES : (c + 1) * LANES] = (centred / (WIN * spread)).astype(BF16)

    spare = jnp.zeros((LANES - GROUPS * BASE, BLOCK), BF16)
    for win in (win0, win1):
        for c in range(chans):
            win[c * LANES + GROUPS * BASE : (c + 1) * LANES, :] = spare

    def fill(e, win):
        first = e // RUN * run_tiles + e % RUN * PER_BLOCK

        def store(row, values):
            win[row : row + BASE, :] = values

        def factor(c):
            return jnp.concatenate([scale[first + q, c : c + 1, :] for q in range(PER_BLOCK)], axis=1)

        fill_windows(base16, first, PER_BLOCK, factor, store)

    def multiply(e, win):
        product = jnp.dot(tmat[...], win[...], preferred_element_type=F32)
        for r in range(per_sta):
            for q in range(PER_BLOCK):
                acc[q, pl.ds(e * per_sta + r, n_sta, stride=n_split * per_sta), :] = product[
                    r * n_sta : (r + 1) * n_sta, q * LANES : (q + 1) * LANES
                ]

    fill(0, win0)

    def two_blocks(i, carry):
        multiply(2 * i, win0)
        fill(2 * i + 1, win1)
        multiply(2 * i + 1, win1)
        fill(2 * i + 2, win0)
        return carry

    lax.fori_loop(0, n_split // 2 - 1, two_blocks, 0)
    multiply(n_split - 2, win0)
    fill(n_split - 1, win1)
    multiply(n_split - 1, win1)
    rows = n_split * per_sta
    for j in range(n_sta):
        for q in range(PER_BLOCK):
            out_ref[j, :, q * LANES : (q + 1) * LANES] = acc[
                q, j * rows : (j + 1) * rows, :
            ].astype(BF16)


def body(record, owner, offset, station, valid):
    ch_dev, samp_dev = record.shape
    n_gather, n_split, n_sta = lax.axis_size(GATHER), lax.axis_size(SPLIT), lax.axis_size(STA)
    chans = ch_dev // n_split
    per_sta = NTPL // n_sta
    runs = n_split // RUN
    wide = runs * (RUN * PER_BLOCK + 1) * LANES

    code = (station * 2 + valid).astype(F32)

    rounded = record.astype(BF16).reshape(n_split, chans, samp_dev)
    mine = lax.all_to_all(rounded, SPLIT, 0, 0, tiled=True)
    mine, code = lax.optimization_barrier((mine, code))
    codes = lax.all_to_all(
        jnp.broadcast_to(code[None, :], (n_sta, ch_dev)), STA, 0, 0, tiled=True
    ).reshape(n_sta * ch_dev // LANES, LANES)
    own = lax.dynamic_slice_in_dim(code, lax.axis_index(SPLIT) * chans, chans)[:, None]
    whole = lax.all_gather(mine, GATHER, axis=0, tiled=False)

    starts = owner[:, 0] * samp_dev + offset
    starts = starts.reshape(NSTEP, n_sta, per_sta // NSTEP).transpose(0, 2, 1).reshape(NTPL)
    group = lax.axis_index(GATHER).astype(jnp.int32).reshape(1)

    part = pl.pallas_call(
        stack_kernel,
        out_shape=jax.ShapeDtypeStruct((n_sta, n_split * per_sta, samp_dev), BF16),
        in_specs=[SMEM, SMEM, VMEM, VMEM, VMEM],
        out_specs=VMEM,
        scratch_shapes=[
            pltpu.VMEM((n_gather * n_split * PER_BLOCK + 1, chans, LANES), F32),
            pltpu.VMEM((chans * NTPL, LANES), F32),
            pltpu.VMEM((NTPL, chans * LANES), BF16),
            pltpu.VMEM((chans * BASE, LANES), F32),
            pltpu.VMEM((wide // LANES, chans * BASE, LANES), BF16),
            pltpu.VMEM((wide // LANES, chans, LANES), F32),
            pltpu.VMEM((chans * LANES, samp_dev), BF16),
            pltpu.VMEM((chans * LANES, samp_dev), BF16),
            pltpu.VMEM((PER_BLOCK, n_split * NTPL, LANES), F32),
        ],
        compiler_params=pltpu.CompilerParams(vmem_limit_bytes=48 * 1024 * 1024),
        cost_estimate=pl.CostEstimate(
            flops=14_000_000_000, bytes_accessed=2 << 20, transcendentals=0
        ),
    )(group, starts, whole, codes, own)

    moved = lax.all_to_all(part, STA, 0, 0, tiled=True)
    summed = jnp.sum(moved.astype(F32), axis=0).reshape(n_split, per_sta, samp_dev)
    final = lax.all_to_all(summed, SPLIT, 0, 0, tiled=True)
    result = jnp.sum(final, axis=0) * (1.0 / 32.0)
    return result.reshape(NSTEP, per_sta // NSTEP, samp_dev)


def solution(mesh):
    fine = Mesh(mesh.devices.reshape(4, 4, 2, 4, 2, 2), TM + STA)
    placed = (P(STA, TM), P(), P(), P(STA), P(STA))
    return jax.shard_map(
        body, mesh=fine, in_specs=placed, out_specs=P(None, STA, TM), check_vma=False
    )
```

```python
import jax
import jax.numpy as jnp
from jax import lax
from jax.experimental import pallas as pl
from jax.experimental.pallas import tpu as pltpu
from jax.sharding import Mesh
from jax.sharding import PartitionSpec as P

WIN = 100
EPSILON = 1e-05
NTPL = 96
NSTEP = 3
TPL_STEP = 32
BLOCK = 512
LANES = 128
PER_BLOCK = BLOCK // LANES
BASE = 16
GROUPS = 7

RUN = 8
TM = ("zh", "zl", "yh")
SPLIT = ("zl", "yh")
GATHER = "zh"
STA = ("x", "yl", "core")

SMEM = pl.BlockSpec(memory_space=pltpu.SMEM)
VMEM = pl.BlockSpec(memory_space=pltpu.VMEM)
F32, BF16 = jnp.float32, jnp.bfloat16


def shift_left(value, by):
    if by == 0:
        return value
    return pltpu.roll(value, value.shape[1] - by, axis=1)


def dot(left, right):
    return jnp.dot(left.astype(BF16), right, preferred_element_type=F32)


def two_parts(value):
    high = value.astype(BF16)
    return high, value - high.astype(F32)


def deviations(values):
    n_tiles, chans, _ = values.shape
    flat = values.reshape(n_tiles * chans, LANES)
    row = lax.broadcasted_iota(jnp.int32, (LANES, LANES), 0)
    lane = lax.broadcasted_iota(jnp.int32, (LANES, LANES), 1)
    own = ((row >= lane) & (row < lane + WIN)).astype(F32).astype(BF16)
    after = (row + LANES < lane + WIN).astype(F32).astype(BF16)

    def window_sum(parts):
        here = sum(dot(part, own) for part in parts).reshape(n_tiles, chans, LANES)
        there = sum(dot(part, after) for part in parts).reshape(n_tiles, chans, LANES)
        return here[:-1] + there[1:]

    mean = window_sum([flat]) / WIN
    square = window_sum(two_parts(flat * flat)) / WIN
    return 1.0 / jnp.sqrt(jnp.maximum(square - mean * mean, 0.0) + EPSILON)


def shifted_base(tile, n_tiles, base32, base16, place, beside):
    chans = tile(0).shape[0]
    lane = lax.broadcasted_iota(jnp.int32, (chans, LANES), 1)
    low = [shift_left(tile(0), i) for i in range(BASE)]
    for q in range(n_tiles):
        if q < n_tiles - 1:
            high = [shift_left(tile(q + 1), i) for i in range(BASE)]
        else:
            high = [jnp.zeros((chans, LANES), F32)] * BASE
        for i in range(BASE):
            base32[pl.ds(i, chans, stride=BASE), :] = jnp.where(lane < LANES - i, low[i], high[i])
        base16[place + q] = base32[...].astype(BF16)
        low = high
        beside(place + q)


def fill_windows(base16, first, count, factor, store):
    chans = base16.shape[1] // BASE
    for c in range(chans):
        piece = jnp.concatenate(
            [base16[first + q, c * BASE : (c + 1) * BASE, :] for q in range(count + 1)], axis=1
        )
        for g in range(GROUPS):
            moved = shift_left(piece, g * BASE)[:, : count * LANES]
            store(c * LANES + g * BASE, (moved.astype(F32) * factor(c)).astype(BF16))


def stack_kernel(
    group_ref, start_ref, rec_ref, codes_ref, own_ref, out_ref,
    tiles, raw, tmat, base32, base16, scale, win0, win1, acc,
):
    n_gather, n_split, chans, _ = rec_ref.shape
    n_sta = out_ref.shape[0]
    per_sta = NTPL // n_sta
    n_runs = n_split // RUN
    run_tiles = RUN * PER_BLOCK + 1

    for l in range(n_gather):
        for h in range(n_runs):
            for y in range(RUN):
                block = (h * n_gather + l) * RUN + y
                for q in range(PER_BLOCK):
                    tiles[block * PER_BLOCK + q] = rec_ref[
                        l, h * RUN + y, :, q * LANES : (q + 1) * LANES
                    ].astype(F32)
    tiles[n_gather * n_split * PER_BLOCK] = jnp.zeros((chans, LANES), F32)

    codes = codes_ref[...].astype(jnp.int32)
    own = own_ref[...].astype(jnp.int32)
    own_station = own // 2
    own_valid = own - own_station * 2
    counts = jnp.zeros((chans, codes.shape[1]), jnp.int32)
    for r in range(codes.shape[0]):
        row = codes[r : r + 1, :]
        station = row // 2
        counts = counts + jnp.where(own_station == station, row - station * 2, 0)
    total = jnp.sum(counts.astype(F32), axis=1, keepdims=True)
    weight = own_valid.astype(F32) / jnp.maximum(total, 1.0)

    for h in range(n_runs):
        first = (h * n_gather + group_ref[0]) * (RUN * PER_BLOCK)
        values = tiles[pl.ds(first, run_tiles)]
        scale[h * run_tiles : (h + 1) * run_tiles - 1] = weight[None] * deviations(values)

    def take_template(row, carry):
        start = start_ref[row]
        tile = start // LANES
        rest = start - tile * LANES
        back = lax.rem(LANES - rest, LANES)
        low = pltpu.roll(tiles[tile], back, axis=1)
        high = pltpu.roll(tiles[tile + 1], back, axis=1)
        lane = lax.broadcasted_iota(jnp.int32, (chans, LANES), 1)
        raw[pl.ds(row, chans, stride=NTPL), :] = jnp.where(lane < LANES - rest, low, high)
        return carry

    lax.fori_loop(0, NTPL, take_template, 0, unroll=96)

    lane = lax.broadcasted_iota(jnp.int32, (NTPL, LANES), 1)
    inside = lane < WIN
    ones = jnp.ones((LANES, LANES), BF16)
    def normalize(c):
        if c >= chans:
            return
        values = jnp.where(inside, raw[c * NTPL : (c + 1) * NTPL, :], 0.0)
        mean = dot(values, ones) / WIN
        centred = jnp.where(inside, values - mean, 0.0)
        total = sum(dot(part, ones) for part in two_parts(centred * centred))
        spread = jnp.sqrt(total / WIN + EPSILON)
        tmat[:, c * LANES : (c + 1) * LANES] = (centred / (WIN * spread)).astype(BF16)

    for h in range(n_runs):
        first = (h * n_gather + group_ref[0]) * (RUN * PER_BLOCK)
        shifted_base(
            lambda q: tiles[first + q], run_tiles, base32, base16, h * run_tiles, normalize
        )

    spare = jnp.zeros((LANES - GROUPS * BASE, BLOCK), BF16)
    for win in (win0, win1):
        for c in range(chans):
            win[c * LANES + GROUPS * BASE : (c + 1) * LANES, :] = spare

    def fill(e, win):
        first = e // RUN * run_tiles + e % RUN * PER_BLOCK

        def store(row, values):
            win[row : row + BASE, :] = values

        def factor(c):
            return jnp.concatenate([scale[first + q, c : c + 1, :] for q in range(PER_BLOCK)], axis=1)

        fill_windows(base16, first, PER_BLOCK, factor, store)

    def multiply(e, win):
        product = jnp.dot(tmat[...], win[...], preferred_element_type=F32)
        for r in range(per_sta):
            for q in range(PER_BLOCK):
                acc[q, pl.ds(e * per_sta + r, n_sta, stride=n_split * per_sta), :] = product[
                    r * n_sta : (r + 1) * n_sta, q * LANES : (q + 1) * LANES
                ]

    fill(0, win0)

    def two_blocks(i):
        multiply(2 * i, win0)
        fill(2 * i + 1, win1)
        multiply(2 * i + 1, win1)
        fill(2 * i + 2, win0)

    for i in range(n_split // 2 - 1):
        two_blocks(i)
    multiply(n_split - 2, win0)
    fill(n_split - 1, win1)
    multiply(n_split - 1, win1)
    rows = n_split * per_sta
    for j in range(n_sta):
        for q in range(PER_BLOCK):
            out_ref[j, :, q * LANES : (q + 1) * LANES] = acc[
                q, j * rows : (j + 1) * rows, :
            ].astype(BF16)


def body(record, owner, offset, station, valid):
    ch_dev, samp_dev = record.shape
    n_gather, n_split, n_sta = lax.axis_size(GATHER), lax.axis_size(SPLIT), lax.axis_size(STA)
    chans = ch_dev // n_split
    per_sta = NTPL // n_sta
    runs = n_split // RUN
    wide = runs * (RUN * PER_BLOCK + 1) * LANES

    code = (station * 2 + valid).astype(F32)

    rounded = record.astype(BF16).reshape(n_split, chans, samp_dev)
    mine = lax.all_to_all(rounded, SPLIT, 0, 0, tiled=True)
    mine, code = lax.optimization_barrier((mine, code))
    codes = lax.all_to_all(
        jnp.broadcast_to(code[None, :], (n_sta, ch_dev)), STA, 0, 0, tiled=True
    ).reshape(n_sta * ch_dev // LANES, LANES)
    own = lax.dynamic_slice_in_dim(code, lax.axis_index(SPLIT) * chans, chans)[:, None]
    whole = lax.all_gather(mine, GATHER, axis=0, tiled=False)

    starts = owner[:, 0] * samp_dev + offset
    starts = starts.reshape(NSTEP, n_sta, per_sta // NSTEP).transpose(0, 2, 1).reshape(NTPL)
    group = lax.axis_index(GATHER).astype(jnp.int32).reshape(1)

    part = pl.pallas_call(
        stack_kernel,
        out_shape=jax.ShapeDtypeStruct((n_sta, n_split * per_sta, samp_dev), BF16),
        in_specs=[SMEM, SMEM, VMEM, VMEM, VMEM],
        out_specs=VMEM,
        scratch_shapes=[
            pltpu.VMEM((n_gather * n_split * PER_BLOCK + 1, chans, LANES), F32),
            pltpu.VMEM((chans * NTPL, LANES), F32),
            pltpu.VMEM((NTPL, chans * LANES), BF16),
            pltpu.VMEM((chans * BASE, LANES), F32),
            pltpu.VMEM((wide // LANES, chans * BASE, LANES), BF16),
            pltpu.VMEM((wide // LANES, chans, LANES), F32),
            pltpu.VMEM((chans * LANES, samp_dev), BF16),
            pltpu.VMEM((chans * LANES, samp_dev), BF16),
            pltpu.VMEM((PER_BLOCK, n_split * NTPL, LANES), F32),
        ],
        compiler_params=pltpu.CompilerParams(vmem_limit_bytes=48 * 1024 * 1024),
        cost_estimate=pl.CostEstimate(
            flops=14_000_000_000, bytes_accessed=2 << 20, transcendentals=0
        ),
    )(group, starts, whole, codes, own)

    moved = lax.all_to_all(part, STA, 0, 0, tiled=True)
    summed = jnp.sum(moved.astype(F32), axis=0).reshape(n_split, per_sta, samp_dev)
    final = lax.all_to_all(summed, SPLIT, 0, 0, tiled=True)
    result = jnp.sum(final, axis=0) * (1.0 / 32.0)
    return result.reshape(NSTEP, per_sta // NSTEP, samp_dev)


def solution(mesh):
    fine = Mesh(mesh.devices.reshape(4, 4, 2, 4, 2, 2), TM + STA)
    placed = (P(STA, TM), P(), P(), P(STA), P(STA))
    return jax.shard_map(
        body, mesh=fine, in_specs=placed, out_specs=P(None, STA, TM), check_vma=False
    )
```

```python
import jax
import jax.numpy as jnp
from jax import lax
from jax.experimental import pallas as pl
from jax.experimental.pallas import tpu as pltpu
from jax.sharding import Mesh
from jax.sharding import PartitionSpec as P

WIN = 100
EPSILON = 1e-05
NTPL = 96
NSTEP = 3
TPL_STEP = 32
BLOCK = 512
LANES = 128
PER_BLOCK = BLOCK // LANES
BASE = 16
GROUPS = 7

RUN = 8
TM = ("zh", "zl", "yh")
SPLIT = ("zl", "yh")
GATHER = "zh"
STA = ("x", "yl", "core")
CHIPS = ("x", "yl")
CORES = 2

SMEM = pl.BlockSpec(memory_space=pltpu.SMEM)
VMEM = pl.BlockSpec(memory_space=pltpu.VMEM)
F32, BF16 = jnp.float32, jnp.bfloat16


def shift_left(value, by):
    if by == 0:
        return value
    return pltpu.roll(value, value.shape[1] - by, axis=1)


def dot(left, right):
    return jnp.dot(left.astype(BF16), right, preferred_element_type=F32)


def two_parts(value):
    high = value.astype(BF16)
    return high, value - high.astype(F32)


def deviations(values):
    n_tiles, chans, _ = values.shape
    flat = values.reshape(n_tiles * chans, LANES)
    row = lax.broadcasted_iota(jnp.int32, (LANES, LANES), 0)
    lane = lax.broadcasted_iota(jnp.int32, (LANES, LANES), 1)
    own = ((row >= lane) & (row < lane + WIN)).astype(F32).astype(BF16)
    after = (row + LANES < lane + WIN).astype(F32).astype(BF16)

    def window_sum(parts):
        here = sum(dot(part, own) for part in parts).reshape(n_tiles, chans, LANES)
        there = sum(dot(part, after) for part in parts).reshape(n_tiles, chans, LANES)
        return here[:-1] + there[1:]

    mean = window_sum([flat]) / WIN
    square = window_sum(two_parts(flat * flat)) / WIN
    return 1.0 / jnp.sqrt(jnp.maximum(square - mean * mean, 0.0) + EPSILON)


def shifted_base(tile, n_tiles, base32, base16, place):
    chans = tile(0).shape[0]
    lane = lax.broadcasted_iota(jnp.int32, (chans, LANES), 1)
    low = [shift_left(tile(0), i) for i in range(BASE)]
    for q in range(n_tiles):
        if q < n_tiles - 1:
            high = [shift_left(tile(q + 1), i) for i in range(BASE)]
        else:
            high = [jnp.zeros((chans, LANES), F32)] * BASE
        for i in range(BASE):
            base32[pl.ds(i, chans, stride=BASE), :] = jnp.where(lane < LANES - i, low[i], high[i])
        base16[place + q] = base32[...].astype(BF16)
        low = high


def fill_windows(base16, first, count, factor, store):
    chans = base16.shape[1] // BASE
    for c in range(chans):
        piece = jnp.concatenate(
            [base16[first + q, c * BASE : (c + 1) * BASE, :] for q in range(count + 1)], axis=1
        )
        for g in range(GROUPS):
            moved = shift_left(piece, g * BASE)[:, : count * LANES]
            store(c * LANES + g * BASE, (moved.astype(F32) * factor(c)).astype(BF16))


def stack_kernel(
    group_ref, start_ref, rec_ref, codes_ref, own_ref, out_ref,
    tiles, raw, tmat, base32, base16, scale, win0, win1, acc,
):
    n_gather, n_split, chans, _ = rec_ref.shape
    n_sta = out_ref.shape[0]
    per_sta = NTPL // n_sta
    n_runs = n_split // RUN
    run_tiles = RUN * PER_BLOCK + 1

    for l in range(n_gather):
        for h in range(n_runs):
            for y in range(RUN):
                block = (h * n_gather + l) * RUN + y
                for q in range(PER_BLOCK):
                    tiles[block * PER_BLOCK + q] = rec_ref[
                        l, h * RUN + y, :, q * LANES : (q + 1) * LANES
                    ].astype(F32)
    tiles[n_gather * n_split * PER_BLOCK] = jnp.zeros((chans, LANES), F32)

    codes = codes_ref[...].astype(jnp.int32)
    own = own_ref[...].astype(jnp.int32)
    own_station = own // 2
    own_valid = own - own_station * 2
    counts = jnp.zeros((chans, codes.shape[1]), jnp.int32)
    for r in range(codes.shape[0]):
        row = codes[r : r + 1, :]
        station = row // 2
        counts = counts + jnp.where(own_station == station, row - station * 2, 0)
    total = jnp.sum(counts.astype(F32), axis=1, keepdims=True)
    weight = own_valid.astype(F32) / jnp.maximum(total, 1.0)

    for h in range(n_runs):
        first = (h * n_gather + group_ref[0]) * (RUN * PER_BLOCK)
        values = tiles[pl.ds(first, run_tiles)]
        scale[h * run_tiles : (h + 1) * run_tiles - 1] = weight[None] * deviations(values)
        shifted_base(lambda q: tiles[first + q], run_tiles, base32, base16, h * run_tiles)

    def take_template(row, carry):
        start = start_ref[row]
        tile = start // LANES
        rest = start - tile * LANES
        back = lax.rem(LANES - rest, LANES)
        low = pltpu.roll(tiles[tile], back, axis=1)
        high = pltpu.roll(tiles[tile + 1], back, axis=1)
        lane = lax.broadcasted_iota(jnp.int32, (chans, LANES), 1)
        raw[pl.ds(row, chans, stride=NTPL), :] = jnp.where(lane < LANES - rest, low, high)
        return carry

    lax.fori_loop(0, NTPL, take_template, 0, unroll=96)

    lane = lax.broadcasted_iota(jnp.int32, (NTPL, LANES), 1)
    inside = lane < WIN
    ones = jnp.ones((LANES, LANES), BF16)
    for c in range(chans):
        values = jnp.where(inside, raw[c * NTPL : (c + 1) * NTPL, :], 0.0)
        mean = dot(values, ones) / WIN
        centred = jnp.where(inside, values - mean, 0.0)
        total = sum(dot(part, ones) for part in two_parts(centred * centred))
        spread = jnp.sqrt(total / WIN + EPSILON)
        tmat[:, c * LANES : (c + 1) * LANES] = (centred / (WIN * spread)).astype(BF16)

    spare = jnp.zeros((LANES - GROUPS * BASE, BLOCK), BF16)
    for win in (win0, win1):
        for c in range(chans):
            win[c * LANES + GROUPS * BASE : (c + 1) * LANES, :] = spare

    def fill(e, win):
        first = e // RUN * run_tiles + e % RUN * PER_BLOCK

        def store(row, values):
            win[row : row + BASE, :] = values

        def factor(c):
            return jnp.concatenate([scale[first + q, c : c + 1, :] for q in range(PER_BLOCK)], axis=1)

        fill_windows(base16, first, PER_BLOCK, factor, store)

    def multiply(e, win):
        product = jnp.dot(tmat[...], win[...], preferred_element_type=F32)
        for r in range(per_sta):
            for q in range(PER_BLOCK):
                acc[q, pl.ds(e * per_sta + r, n_sta, stride=n_split * per_sta), :] = product[
                    r * n_sta : (r + 1) * n_sta, q * LANES : (q + 1) * LANES
                ]

    fill(0, win0)

    def two_blocks(i, carry):
        multiply(2 * i, win0)
        fill(2 * i + 1, win1)
        multiply(2 * i + 1, win1)
        fill(2 * i + 2, win0)
        return carry

    lax.fori_loop(0, n_split // 2 - 1, two_blocks, 0)
    multiply(n_split - 2, win0)
    fill(n_split - 1, win1)
    multiply(n_split - 1, win1)
    rows = n_split * per_sta
    for j in range(n_sta):
        place = j % CORES * (n_sta // CORES) + j // CORES
        for q in range(PER_BLOCK):
            out_ref[place, :, q * LANES : (q + 1) * LANES] = acc[
                q, j * rows : (j + 1) * rows, :
            ].astype(BF16)


def body(record, owner, offset, station, valid):
    ch_dev, samp_dev = record.shape
    n_gather, n_split, n_sta = lax.axis_size(GATHER), lax.axis_size(SPLIT), lax.axis_size(STA)
    chans = ch_dev // n_split
    per_sta = NTPL // n_sta
    runs = n_split // RUN
    wide = runs * (RUN * PER_BLOCK + 1) * LANES

    code = (station * 2 + valid).astype(F32)

    rounded = record.astype(BF16).reshape(n_split, chans, samp_dev)
    mine = lax.all_to_all(rounded, SPLIT, 0, 0, tiled=True)
    mine, code = lax.optimization_barrier((mine, code))
    codes = lax.all_to_all(
        jnp.broadcast_to(code[None, :], (n_sta, ch_dev)), STA, 0, 0, tiled=True
    ).reshape(n_sta * ch_dev // LANES, LANES)
    own = lax.dynamic_slice_in_dim(code, lax.axis_index(SPLIT) * chans, chans)[:, None]
    whole = lax.all_gather(mine, GATHER, axis=0, tiled=False)

    starts = owner[:, 0] * samp_dev + offset
    starts = starts.reshape(NSTEP, n_sta, per_sta // NSTEP).transpose(0, 2, 1).reshape(NTPL)
    group = lax.axis_index(GATHER).astype(jnp.int32).reshape(1)

    part = pl.pallas_call(
        stack_kernel,
        out_shape=jax.ShapeDtypeStruct((n_sta, n_split * per_sta, samp_dev), BF16),
        in_specs=[SMEM, SMEM, VMEM, VMEM, VMEM],
        out_specs=VMEM,
        scratch_shapes=[
            pltpu.VMEM((n_gather * n_split * PER_BLOCK + 1, chans, LANES), F32),
            pltpu.VMEM((chans * NTPL, LANES), F32),
            pltpu.VMEM((NTPL, chans * LANES), BF16),
            pltpu.VMEM((chans * BASE, LANES), F32),
            pltpu.VMEM((wide // LANES, chans * BASE, LANES), BF16),
            pltpu.VMEM((wide // LANES, chans, LANES), F32),
            pltpu.VMEM((chans * LANES, samp_dev), BF16),
            pltpu.VMEM((chans * LANES, samp_dev), BF16),
            pltpu.VMEM((PER_BLOCK, n_split * NTPL, LANES), F32),
        ],
        compiler_params=pltpu.CompilerParams(vmem_limit_bytes=48 * 1024 * 1024),
        cost_estimate=pl.CostEstimate(
            flops=14_000_000_000, bytes_accessed=2 << 20, transcendentals=0
        ),
    )(group, starts, whole, codes, own)

    pair = lax.all_to_all(part, "core", 0, 0, tiled=True)
    pair = pair.reshape(CORES, n_sta // CORES, n_split * per_sta, samp_dev)
    half = jnp.sum(pair.astype(F32), axis=0).astype(BF16)
    moved = lax.all_to_all(half, CHIPS, 0, 0, tiled=True)
    summed = jnp.sum(moved.astype(F32), axis=0).reshape(n_split, per_sta, samp_dev)
    final = lax.all_to_all(summed, SPLIT, 0, 0, tiled=True)
    result = jnp.sum(final, axis=0) * (1.0 / 32.0)
    return result.reshape(NSTEP, per_sta // NSTEP, samp_dev)


def solution(mesh):
    fine = Mesh(mesh.devices.reshape(4, 4, 2, 4, 2, 2), TM + STA)
    placed = (P(STA, TM), P(), P(), P(STA), P(STA))
    return jax.shard_map(
        body, mesh=fine, in_specs=placed, out_specs=P(None, STA, TM), check_vma=False
    )
```

```python
import jax
import jax.numpy as jnp
from jax import lax
from jax.experimental import pallas as pl
from jax.experimental.pallas import tpu as pltpu
from jax.sharding import Mesh
from jax.sharding import PartitionSpec as P

WIN = 100
EPSILON = 1e-05
NTPL = 96
NSTEP = 3
TPL_STEP = 32
BLOCK = 512
LANES = 128
PER_BLOCK = BLOCK // LANES
BASE = 16
GROUPS = 7

RUN = 8
TM = ("zh", "zl", "yh")
SPLIT = ("zl", "yh")
GATHER = "zh"
STA = ("x", "yl", "core")

SMEM = pl.BlockSpec(memory_space=pltpu.SMEM)
VMEM = pl.BlockSpec(memory_space=pltpu.VMEM)
F32, BF16 = jnp.float32, jnp.bfloat16


def shift_left(value, by):
    if by == 0:
        return value
    return pltpu.roll(value, value.shape[1] - by, axis=1)


def dot(left, right):
    return jnp.dot(left.astype(BF16), right, preferred_element_type=F32)


def two_parts(value):
    high = value.astype(BF16)
    return high, value - high.astype(F32)


def deviations(values):
    n_tiles, chans, _ = values.shape
    flat = values.reshape(n_tiles * chans, LANES)
    row = lax.broadcasted_iota(jnp.int32, (LANES, LANES), 0)
    lane = lax.broadcasted_iota(jnp.int32, (LANES, LANES), 1)
    own = ((row >= lane) & (row < lane + WIN)).astype(F32).astype(BF16)
    after = (row + LANES < lane + WIN).astype(F32).astype(BF16)

    def window_sum(parts):
        here = sum(dot(part, own) for part in parts).reshape(n_tiles, chans, LANES)
        there = sum(dot(part, after) for part in parts).reshape(n_tiles, chans, LANES)
        return here[:-1] + there[1:]

    mean = window_sum([flat]) / WIN
    square = window_sum(two_parts(flat * flat)) / WIN
    return 1.0 / jnp.sqrt(jnp.maximum(square - mean * mean, 0.0) + EPSILON)


def shifted_base(tile, n_tiles, base32, base16, place):
    chans = tile(0).shape[0]
    lane = lax.broadcasted_iota(jnp.int32, (chans, LANES), 1)
    low = [shift_left(tile(0), i) for i in range(BASE)]
    for q in range(n_tiles):
        if q < n_tiles - 1:
            high = [shift_left(tile(q + 1), i) for i in range(BASE)]
        else:
            high = [jnp.zeros((chans, LANES), F32)] * BASE
        for i in range(BASE):
            base32[pl.ds(i, chans, stride=BASE), :] = jnp.where(lane < LANES - i, low[i], high[i])
        base16[place + q] = base32[...].astype(BF16)
        low = high


def fill_windows(base16, first, count, factor, store):
    chans = base16.shape[1] // BASE
    for c in range(chans):
        piece = jnp.concatenate(
            [base16[first + q, c * BASE : (c + 1) * BASE, :] for q in range(count + 1)], axis=1
        )
        for g in range(GROUPS):
            moved = shift_left(piece, g * BASE)[:, : count * LANES]
            store(c * LANES + g * BASE, (moved.astype(F32) * factor(c)).astype(BF16))


def stack_kernel(
    group_ref, start_ref, rec_ref, codes_ref, own_ref, out_ref,
    tiles, raw, tmat, base32, base16, scale, win0, win1, acc,
):
    n_gather, n_split, chans, _ = rec_ref.shape
    n_sta = out_ref.shape[0]
    per_sta = NTPL // n_sta
    n_runs = n_split // RUN
    run_tiles = RUN * PER_BLOCK + 1

    for l in range(n_gather):
        for h in range(n_runs):
            for y in range(RUN):
                block = (h * n_gather + l) * RUN + y
                for q in range(PER_BLOCK):
                    tiles[block * PER_BLOCK + q] = rec_ref[
                        l, h * RUN + y, :, q * LANES : (q + 1) * LANES
                    ].astype(F32)
    tiles[n_gather * n_split * PER_BLOCK] = jnp.zeros((chans, LANES), F32)

    codes = codes_ref[...].astype(jnp.int32)
    own = own_ref[...].astype(jnp.int32)
    own_station = own // 2
    own_valid = own - own_station * 2
    counts = jnp.zeros((chans, codes.shape[1]), jnp.int32)
    for r in range(codes.shape[0]):
        row = codes[r : r + 1, :]
        station = row // 2
        counts = counts + jnp.where(own_station == station, row - station * 2, 0)
    total = jnp.sum(counts.astype(F32), axis=1, keepdims=True)
    weight = own_valid.astype(F32) / jnp.maximum(total, 1.0)

    for h in range(n_runs):
        first = (h * n_gather + group_ref[0]) * (RUN * PER_BLOCK)
        values = tiles[pl.ds(first, run_tiles)]
        scale[h * run_tiles : (h + 1) * run_tiles - 1] = weight[None] * deviations(values)
        shifted_base(lambda q: tiles[first + q], run_tiles, base32, base16, h * run_tiles)

    def take_template(row, carry):
        start = start_ref[row]
        tile = start // LANES
        rest = start - tile * LANES
        back = lax.rem(LANES - rest, LANES)
        low = pltpu.roll(tiles[tile], back, axis=1)
        high = pltpu.roll(tiles[tile + 1], back, axis=1)
        lane = lax.broadcasted_iota(jnp.int32, (chans, LANES), 1)
        raw[pl.ds(row, chans, stride=NTPL), :] = jnp.where(lane < LANES - rest, low, high)
        return carry

    lax.fori_loop(0, NTPL, take_template, 0, unroll=96)

    lane = lax.broadcasted_iota(jnp.int32, (NTPL, LANES), 1)
    inside = lane < WIN
    ones = jnp.ones((LANES, LANES), BF16)
    for c in range(chans):
        values = jnp.where(inside, raw[c * NTPL : (c + 1) * NTPL, :], 0.0)
        mean = dot(values, ones) / WIN
        centred = jnp.where(inside, values - mean, 0.0)
        total = sum(dot(part, ones) for part in two_parts(centred * centred))
        spread = jnp.sqrt(total / WIN + EPSILON)
        tmat[:, c * LANES : (c + 1) * LANES] = (centred / (WIN * spread)).astype(BF16)

    spare = jnp.zeros((LANES - GROUPS * BASE, BLOCK), BF16)
    for win in (win0, win1):
        for c in range(chans):
            win[c * LANES + GROUPS * BASE : (c + 1) * LANES, :] = spare

    def fill(e, win):
        first = e // RUN * run_tiles + e % RUN * PER_BLOCK

        def store(row, values):
            win[row : row + BASE, :] = values

        def factor(c):
            return jnp.concatenate([scale[first + q, c : c + 1, :] for q in range(PER_BLOCK)], axis=1)

        fill_windows(base16, first, PER_BLOCK, factor, store)

    def multiply(e, win):
        product = jnp.dot(tmat[...], win[...], preferred_element_type=F32)
        for r in range(per_sta):
            for q in range(PER_BLOCK):
                acc[q, pl.ds(e * per_sta + r, n_sta, stride=n_split * per_sta), :] = product[
                    r * n_sta : (r + 1) * n_sta, q * LANES : (q + 1) * LANES
                ]

    fill(0, win0)

    def two_blocks(i, carry):
        multiply(2 * i, win0)
        fill(2 * i + 1, win1)
        multiply(2 * i + 1, win1)
        fill(2 * i + 2, win0)
        return carry

    lax.fori_loop(0, n_split // 2 - 1, two_blocks, 0)
    multiply(n_split - 2, win0)
    fill(n_split - 1, win1)
    multiply(n_split - 1, win1)
    rows = n_split * per_sta
    for j in range(n_sta):
        for q in range(PER_BLOCK):
            out_ref[j, :, q * LANES : (q + 1) * LANES] = acc[
                q, j * rows : (j + 1) * rows, :
            ].astype(BF16)


def body(record, owner, offset, station, valid):
    ch_dev, samp_dev = record.shape
    n_gather, n_split, n_sta = lax.axis_size(GATHER), lax.axis_size(SPLIT), lax.axis_size(STA)
    chans = ch_dev // n_split
    per_sta = NTPL // n_sta
    runs = n_split // RUN
    wide = runs * (RUN * PER_BLOCK + 1) * LANES

    code = (station * 2 + valid).astype(F32)

    rounded = record.astype(BF16).reshape(n_split, chans, samp_dev)
    mine = lax.all_to_all(rounded, SPLIT, 0, 0, tiled=True)
    mine, code = lax.optimization_barrier((mine, code))
    codes = lax.all_to_all(
        jnp.broadcast_to(code[None, :], (n_sta, ch_dev)), STA, 0, 0, tiled=True
    ).reshape(n_sta * ch_dev // LANES, LANES)
    own = lax.dynamic_slice_in_dim(code, lax.axis_index(SPLIT) * chans, chans)[:, None]
    whole = lax.all_gather(mine, GATHER, axis=0, tiled=False)

    starts = owner[:, 0] * samp_dev + offset
    starts = starts.reshape(NSTEP, n_sta, per_sta // NSTEP).transpose(0, 2, 1).reshape(NTPL)
    group = lax.axis_index(GATHER).astype(jnp.int32).reshape(1)

    part = pl.pallas_call(
        stack_kernel,
        out_shape=jax.ShapeDtypeStruct((n_sta, n_split * per_sta, samp_dev), BF16),
        in_specs=[SMEM, SMEM, VMEM, VMEM, VMEM],
        out_specs=VMEM,
        scratch_shapes=[
            pltpu.VMEM((n_gather * n_split * PER_BLOCK + 1, chans, LANES), F32),
            pltpu.VMEM((chans * NTPL, LANES), F32),
            pltpu.VMEM((NTPL, chans * LANES), BF16),
            pltpu.VMEM((chans * BASE, LANES), F32),
            pltpu.VMEM((wide // LANES, chans * BASE, LANES), BF16),
            pltpu.VMEM((wide // LANES, chans, LANES), F32),
            pltpu.VMEM((chans * LANES, samp_dev), BF16),
            pltpu.VMEM((chans * LANES, samp_dev), BF16),
            pltpu.VMEM((PER_BLOCK, n_split * NTPL, LANES), F32),
        ],
        compiler_params=pltpu.CompilerParams(vmem_limit_bytes=48 * 1024 * 1024),
        cost_estimate=pl.CostEstimate(
            flops=14_000_000_000, bytes_accessed=2 << 20, transcendentals=0
        ),
    )(group, starts, whole, codes, own)

    moved = lax.all_to_all(part, STA, 0, 0, tiled=True)
    summed = jnp.sum(moved.astype(F32), axis=0).reshape(n_split, per_sta, samp_dev)
    final = lax.all_to_all(summed.astype(BF16), SPLIT, 0, 0, tiled=True)
    result = jnp.sum(final.astype(F32), axis=0) * (1.0 / 32.0)
    return result.reshape(NSTEP, per_sta // NSTEP, samp_dev)


def solution(mesh):
    fine = Mesh(mesh.devices.reshape(4, 4, 2, 4, 2, 2), TM + STA)
    placed = (P(STA, TM), P(), P(), P(STA), P(STA))
    return jax.shard_map(
        body, mesh=fine, in_specs=placed, out_specs=P(None, STA, TM), check_vma=False
    )
```
